32 devices in a mesh: row: 2 (over x), col: 4 (over z), depth: 4 (over y, core).
Axes of the slice: x: 2, y: 2, z: 4, core: 2. Of those that a mesh axis runs over, the one named last changes fastest.
Arguments:
- tokens: bfloat16 [256, 8192], P(('col', 'depth'), 'row'), may hold values from -6 to 6
- gate_weight: bfloat16 [8192, 14336], P('row', ('col', 'depth')), may hold values from -0.109375 to 0.109375
- up_weight: bfloat16 [8192, 14336], P('row', ('col', 'depth')), may hold values from -0.109375 to 0.109375
- down_weight: bfloat16 [14336, 8192], P(('col', 'depth'), 'row'), may hold values from -0.078125 to 0.078125
- gate_mask: int32 [64, 112], P('row', ('col', 'depth')), may hold values 0 or 1
- up_mask: int32 [64, 112], P('row', ('col', 'depth')), may hold values 0 or 1
- down_mask: int32 [112, 64], P(('col', 'depth'), 'row'), may hold values 0 or 1
- grad_out: bfloat16 [256, 8192], P(('col', 'depth'), 'row'), may hold values from -1.5 to 1.5
Outputs:
- mixed: bfloat16 [256, 8192], P(('col', 'depth'), 'row')
- grad_tokens: bfloat16 [256, 8192], P(('col', 'depth'), 'row')
- grad_gate_weight: bfloat16 [8192, 14336], P('row', ('col', 'depth'))
- grad_up_weight: bfloat16 [8192, 14336], P('row', ('col', 'depth'))
- grad_down_weight: bfloat16 [14336, 8192], P(('col', 'depth'), 'row')
The draws below stay inside these ranges and needn't reach their ends.
Inputs may be any that keep to these rules, and one draw needn't show every extreme that they name: `gate_mask`: 1 keeps the 128 x 128 block of the gate projection, 0 zeroes it. `up_mask`: 1 keeps the 128 x 128 block of the up projection, 0 zeroes it. `down_mask`: 1 keeps the 128 x 128 block of the down projection, 0 zeroes it.
All inputs are finite; a program needn't handle non-finite values.
Results may differ from the reference program's by a relative error of at most 0.015.
Values may be sent and summed in bfloat16 or wider, within the bound.
A program may use at most 128 MiB of HBM per device.

```python
import jax
import jax.numpy as jnp
from jax import lax

D = 8192
FF = 14336
BLK = 128
TOKENS = 256


def plant(result, rng, least, high):
    longest = result.shape.index(max(result.shape))
    spots = []
    for shift in (0, 1):
        where = [jax.random.randint(jax.random.fold_in(rng, axis), (), 0, length) for axis, length in enumerate(result.shape)]
        where[longest] = (where[longest] + shift) % result.shape[longest]
        spots.append(tuple(where))
    return result.at[spots[0]].set(least).at[spots[1]].set(high)


def block_levels(key, shape, pieces, low, largest):
    def one(position, parts):
        draws = jax.random.uniform(jax.random.fold_in(jax.random.fold_in(key, 6), position), (parts,), jnp.float32, low / len(pieces), largest / len(pieces))
        return jnp.repeat(jnp.exp(draws), shape[position] // parts).reshape((-1,) + (1,) * (len(shape) - position - 1))

    level = one(*pieces[0])
    for cut in pieces[1:]:
        level = level * one(*cut)
    return level


def bell_draw(stream_key, dims, deviation, bound, cuts=(), held_as=jnp.bfloat16):
    array = jax.random.normal(stream_key, dims, jnp.float32) * deviation
    if len(cuts) > 0:
        array = block_levels(stream_key, dims, cuts, -0.22, 0.18) * array
    return jnp.clip(array, min=-bound, max=bound).astype(held_as)


def setup_inputs(seed: int = 0) -> dict:
    keys = jax.random.split(jax.random.key(seed), 9)
    tokens = bell_draw(keys[0], (TOKENS, D), 1.0, 6.0, ((0, 16), (1, 2)))
    gate_weight = bell_draw(keys[1], (D, FF), (2 * D // 5) ** -0.5, 0.109375, ((0, 2), (1, 16)))
    up_weight = bell_draw(keys[2], (D, FF), (2 * D // 5) ** -0.5, 0.109375, ((0, 2), (1, 16)))
    down_weight = bell_draw(keys[3], (FF, D), (2 * FF // 5) ** -0.5, 0.078125, ((0, 16), (1, 2)))
    gate_mask = plant((jax.random.randint(keys[4], (D // BLK, FF // BLK), 0, 5) < 2).astype(jnp.int32), jax.random.fold_in(keys[4], 1), 0, 1)
    up_mask = plant((jax.random.randint(keys[5], (D // BLK, FF // BLK), 0, 5) < 2).astype(jnp.int32), jax.random.fold_in(keys[5], 1), 0, 1)
    down_mask = plant((jax.random.randint(keys[6], (FF // BLK, D // BLK), 0, 5) < 2).astype(jnp.int32), jax.random.fold_in(keys[6], 1), 0, 1)
    grad_out = bell_draw(keys[7], (TOKENS, D), 0.25, 1.5, ((0, 16), (1, 2)))
    return dict(tokens=tokens, gate_weight=gate_weight, up_weight=up_weight, down_weight=down_weight, gate_mask=gate_mask, up_mask=up_mask, down_mask=down_mask, grad_out=grad_out)


def expand(mask):
    return jnp.repeat(jnp.repeat(mask, BLK, axis=0), BLK, axis=1) > 0


def reference(tokens, gate_weight, up_weight, down_weight, gate_mask, up_mask, down_mask, grad_out):
    keep_gate = expand(gate_mask)
    keep_up = expand(up_mask)
    keep_down = expand(down_mask)
    kept_gate = jnp.where(keep_gate, gate_weight, jnp.zeros_like(gate_weight))
    kept_up = jnp.where(keep_up, up_weight, jnp.zeros_like(up_weight))
    kept_down = jnp.where(keep_down, down_weight, jnp.zeros_like(down_weight))
    gate = jnp.dot(tokens, kept_gate, preferred_element_type=jnp.float32)
    up = jnp.dot(tokens, kept_up, preferred_element_type=jnp.float32)
    sig = jax.nn.sigmoid(gate)
    act = (gate * sig * up).astype(jnp.bfloat16)
    mixed = jnp.dot(act, kept_down, preferred_element_type=jnp.float32).astype(jnp.bfloat16)
    inner = (((0,), (0,)), ((), ()))
    outer = (((1,), (1,)), ((), ()))
    grad_down = lax.dot_general(act, grad_out, inner, preferred_element_type=jnp.float32)
    grad_down_weight = jnp.where(keep_down, grad_down, jnp.float32(0.0)).astype(jnp.bfloat16)
    grad_act = lax.dot_general(grad_out, kept_down, outer, preferred_element_type=jnp.float32)
    grad_gate = (grad_act * up * sig * (1.0 + gate * (1.0 - sig))).astype(jnp.bfloat16)
    grad_up = (grad_act * gate * sig).astype(jnp.bfloat16)
    grad_g = lax.dot_general(tokens, grad_gate, inner, preferred_element_type=jnp.float32)
    grad_u = lax.dot_general(tokens, grad_up, inner, preferred_element_type=jnp.float32)
    grad_gate_weight = jnp.where(keep_gate, grad_g, jnp.float32(0.0)).astype(jnp.bfloat16)
    grad_up_weight = jnp.where(keep_up, grad_u, jnp.float32(0.0)).astype(jnp.bfloat16)
    grad_in = lax.dot_general(grad_gate, kept_gate, outer, preferred_element_type=jnp.float32)
    grad_in = grad_in + lax.dot_general(grad_up, kept_up, outer, preferred_element_type=jnp.float32)
    grad_tokens = grad_in.astype(jnp.bfloat16)
    return (mixed, grad_tokens, grad_gate_weight, grad_up_weight, grad_down_weight)
```

```python
import functools

import jax
import jax.numpy as jnp
from jax import lax
from jax.experimental import pallas as pl
from jax.experimental.pallas import tpu as pltpu
from jax.sharding import PartitionSpec as P

BLK = 128
PAIR = 2 * BLK
NCH = 4
F32 = jnp.float32
BF16 = jnp.bfloat16
MESH = pl.DeviceIdType.MESH
NT = (((1,), (1,)), ((), ()))
TN = (((0,), (0,)), ((), ()))


def masked(block, row):
    rows, lanes = block.shape
    keep = jnp.broadcast_to(row, (16, lanes)).astype(BF16)
    return (block.reshape(rows // 16, 16, lanes) * keep[None]).reshape(rows, lanes)


def fused(
    R, C,
    x_hbm, g_hbm, wg_hbm, wu_hbm, wd_hbm, kcat, kd,
    mixed, gtok, x_out, g_out, act_out, gc_out,
    x_all, g_all, wcat, wd, act, gc, hf, hb, hr, gf, gb, gr, part, r1, s1, r2, zb, r3,
    a_ss, a_rs, w_sem, h_ss, h_rs, act_ss, act_rs, ga_ss, ga_rs, gc_ss, gc_rs, q_ss, q_rs, o_sem,
):
    r, c, d = lax.axis_index("row"), lax.axis_index("col"), lax.axis_index("depth")
    rows, dl = x_hbm.shape
    tokens = x_all.shape[0]
    nj = wd.shape[0] // BLK
    ni = dl // BLK
    half = tokens // R
    ch = dl // NCH
    d1 = d + 1 - 2 * lax.rem(d, 2)
    d2 = lax.rem(d + 2, 4)
    d3 = lax.rem(d1 + 2, 4)
    own = pl.ds(pl.multiple_of(r * half, half), half)

    def remote(src, dst, ss, rs, dev):
        return pltpu.make_async_remote_copy(
            src_ref=src, dst_ref=dst, send_sem=ss, recv_sem=rs, device_id=dev, device_id_type=MESH
        )

    def col_at(k):
        return lax.rem(c + k, C)

    def row_at(k):
        return lax.rem(r + k, R)

    barrier = pltpu.get_barrier_semaphore()
    peers = [{"col": col_at(k)} for k in range(1, C)]
    peers += [{"row": row_at(k)} for k in range(1, R)]
    peers += [{"depth": d1}, {"depth": d2}]
    for dev in peers:
        pl.semaphore_signal(barrier, inc=1, device_id=dev, device_id_type=MESH)
    pl.semaphore_wait(barrier, len(peers))

    srcs, alls = (x_hbm, g_hbm), (x_all, g_all)

    def blk(cc, dd):
        return pl.ds(pl.multiple_of((cc * 4 + dd) * rows, rows), rows)

    def gather(a, slot, k):
        if slot == 0:
            dev, at = {"col": col_at(k)}, blk(c, d)
        elif slot == 1:
            dev, at = {"depth": d2}, blk(col_at(C - k), d)
        elif slot == 2:
            dev, at = {"depth": d1}, blk(col_at(C - k), d)
        else:
            dev, at = {"depth": d1}, blk(col_at(C - k), d2)
        src = srcs[a] if slot == 0 or (k == 0 and slot < 3) else alls[a].at[at]
        return remote(src, alls[a].at[at], a_ss.at[a, slot, k], a_rs.at[a, slot, k], dev)

    def arrived(a, slot, k):
        dd = (d, d2, d1, d3)[slot]
        at = blk(col_at(C - k), dd)
        remote(
            alls[a].at[at], alls[a].at[at], a_ss.at[a, slot, k], a_rs.at[a, slot, k], {"depth": d1}
        ).wait_recv()

    def local_own(a):
        return pltpu.make_async_copy(srcs[a], alls[a].at[blk(c, d)], o_sem.at[a])

    def gather_first(a):
        for k in range(C - 1, 0, -1):
            gather(a, 0, k).start()
        gather(a, 1, 0).start()
        gather(a, 2, 0).start()
        local_own(a).start()

    def gather_second(a):
        for k in range(1, C):
            arrived(a, 0, k)
            gather(a, 1, k).start()
            gather(a, 2, k).start()

    def gather_third(a):
        for k in range(C):
            arrived(a, 1, k)
            gather(a, 3, k).start()

    def gather_last(a):
        local_own(a).wait()
        for k in range(C):
            arrived(a, 2, k)
        for k in range(C):
            arrived(a, 3, k)

    def lanes(j, width):
        return pl.ds(pl.multiple_of(j * width, width), width)

    def w_copies(j):
        left = pl.ds(pl.multiple_of(j * PAIR, BLK), BLK)
        right = pl.ds(pl.multiple_of(j * PAIR + BLK, BLK), BLK)
        return (
            pltpu.make_async_copy(wg_hbm.at[:, lanes(j, BLK)], wcat.at[:, left], w_sem.at[0, j]),
            pltpu.make_async_copy(wu_hbm.at[:, lanes(j, BLK)], wcat.at[:, right], w_sem.at[1, j]),
        )

    def d_copy(j):
        return pltpu.make_async_copy(
            wd_hbm.at[lanes(j, BLK), :], wd.at[lanes(j, BLK), :], w_sem.at[2, j]
        )

    gather_first(0)
    for j in range(nj):
        for copy in w_copies(j):
            copy.start()
    for j in range(nj):
        d_copy(j).start()

    def mask_cat(j, carry):
        for copy in w_copies(j):
            copy.wait()
        cols = lanes(j, PAIR)

        def one(i, inner):
            at = lanes(i, BLK)
            wcat[at, cols] = masked(wcat[at, cols], kcat[pl.ds(i, 1), cols])
            return inner

        return lax.fori_loop(0, ni, one, carry)

    def mask_down(j, carry):
        d_copy(j).wait()

        def one(i, inner):
            at = lanes(i, dl // NCH)
            wd[lanes(j, BLK), at] = masked(wd[lanes(j, BLK), at], kd[pl.ds(j, 1), at])
            return inner

        return lax.fori_loop(0, NCH, one, carry)

    gather_second(0)
    gather_first(1)
    lax.fori_loop(0, nj, mask_cat, 0)
    gather_third(0)
    lax.fori_loop(0, nj, mask_down, 0)
    gather_last(0)

    def h_send(j, k):
        at = pl.ds(pl.multiple_of(row_at(k) * half, half), half)
        return remote(
            hb.at[at, lanes(j, PAIR)], hr.at[k - 1, :, lanes(j, PAIR)],
            h_ss.at[k - 1, j], h_rs.at[k - 1, j], {"row": row_at(k)},
        )

    def hidden(j, carry):
        cols = lanes(j, PAIR)
        value = jnp.dot(x_all[...], wcat[:, cols], preferred_element_type=F32)
        hf[:, cols] = value
        hb[:, cols] = value.astype(BF16)
        for k in range(1, R):
            h_send(j, k).start()
        return carry

    lax.fori_loop(0, nj, hidden, 0)
    x_copy = pltpu.make_async_copy(x_all, x_out, o_sem.at[2])
    x_copy.start()
    gather_second(1)

    def act_send(j, k):
        at = act.at[own, lanes(j, BLK)]
        return remote(at, at, act_ss.at[k - 1, j], act_rs.at[k - 1, j], {"row": row_at(k)})

    def activate(j, carry):
        cols = lanes(j, PAIR)
        total = hf[own, cols]
        for k in range(1, R):
            h_send(j, k).wait_recv()
            total = total + hr[k - 1, :, cols].astype(F32)
        hf[own, cols] = total
        gate, up = total[:, :BLK], total[:, BLK:]
        act[own, lanes(j, BLK)] = (gate * jax.nn.sigmoid(gate) * up).astype(BF16)
        for k in range(1, R):
            act_send(j, k).start()
        return carry

    lax.fori_loop(0, nj, activate, 0)
    gather_third(1)
    gather_last(1)
    g_copy = pltpu.make_async_copy(g_all, g_out, o_sem.at[3])
    g_copy.start()

    def ga_send(j, k):
        at = pl.ds(pl.multiple_of(row_at(k) * half, half), half)
        return remote(
            gb.at[at, lanes(j, BLK)], gr.at[k - 1, :, lanes(j, BLK)],
            ga_ss.at[k - 1, j], ga_rs.at[k - 1, j], {"row": row_at(k)},
        )

    def back(j, carry):
        cols = lanes(j, BLK)
        value = lax.dot_general(g_all[...], wd[cols, :], NT, preferred_element_type=F32)
        gf[:, cols] = value
        gb[:, cols] = value.astype(BF16)
        for k in range(1, R):
            ga_send(j, k).start()
        return carry

    lax.fori_loop(0, nj, back, 0)

    def peer_rows(k):
        return pl.ds(pl.multiple_of(row_at(R - k) * half, half), half)

    def act_wait(j, carry):
        for k in range(1, R):
            at = act.at[peer_rows(k), lanes(j, BLK)]
            remote(at, at, act_ss.at[k - 1, j], act_rs.at[k - 1, j], {"row": row_at(k)}).wait_recv()
        return carry

    lax.fori_loop(0, nj, act_wait, 0)
    act_copy = pltpu.make_async_copy(act, act_out, o_sem.at[4])
    act_copy.start()

    outs = (mixed, gtok)

    def send1(a, q, h):
        cols = pl.ds(q * ch, ch)
        dst = (d1, d3)[h]
        return remote(
            part.at[a, dst, :, cols], r1.at[a, h, :, cols],
            q_ss.at[a, q, h], q_rs.at[a, q, h], {"depth": d1},
        )

    def send2(a, q):
        cols = pl.ds(q * ch, ch)
        return remote(
            s1.at[a, :, cols], r2.at[a, :, cols], q_ss.at[a, q, 2], q_rs.at[a, q, 2], {"depth": d2}
        )

    def send3(a, q, k):
        cols = pl.ds(q * ch, ch)
        at = pl.ds(pl.multiple_of(col_at(k) * rows, rows), rows)
        return remote(
            zb.at[a, at, cols], r3.at[a, k - 1, :, cols],
            q_ss.at[a, q, 2 + k], q_rs.at[a, q, 2 + k], {"col": col_at(k)},
        )

    def stage_a(a, q):
        def tile(n, carry):
            cols = pl.ds(pl.multiple_of(q * ch + n * PAIR, PAIR), PAIR)
            if a == 0:
                value = jnp.dot(act[...], wd[:, cols], preferred_element_type=F32)
            else:
                value = lax.dot_general(gc[...], wcat[cols, :], NT, preferred_element_type=F32)
            value = value.astype(BF16)
            for cc in range(C):
                for dd in range(4):
                    at = (cc * 4 + dd) * rows
                    part[a, dd, cc * rows : (cc + 1) * rows, cols] = value[at : at + rows]
            return carry

        lax.fori_loop(0, ch // PAIR, tile, 0)
        send1(a, q, 1).start()
        send1(a, q, 0).start()

    def stage_b(a, q):
        cols = pl.ds(q * ch, ch)
        send1(a, q, 1).wait_recv()
        s1[a, :, cols] = (part[a, d2, :, cols].astype(F32) + r1[a, 1, :, cols].astype(F32)).astype(BF16)
        send2(a, q).start()

    def stage_c(a, q):
        cols = pl.ds(q * ch, ch)
        send1(a, q, 0).wait_recv()
        send2(a, q).wait_recv()
        total = part[a, d, :, cols].astype(F32) + r1[a, 0, :, cols].astype(F32)
        zb[a, :, cols] = (total + r2[a, :, cols].astype(F32)).astype(BF16)
        for k in range(C - 1, 0, -1):
            send3(a, q, k).start()

    def stage_d(a, q):
        cols = pl.ds(q * ch, ch)
        at = pl.ds(pl.multiple_of(c * rows, rows), rows)
        total = zb[a, at, cols].astype(F32)
        for k in range(1, C):
            send3(a, q, k).wait_recv()
            total = total + r3[a, k - 1, :, cols].astype(F32)
        outs[a][:, cols] = total.astype(BF16)

    for q in range(NCH):
        stage_a(0, q)
        if q > 0:
            stage_b(0, q - 1)
    stage_b(0, NCH - 1)

    def gc_send(j, k):
        at = gc.at[own, lanes(j, PAIR)]
        return remote(at, at, gc_ss.at[k - 1, j], gc_rs.at[k - 1, j], {"row": row_at(k)})

    def swiglu_back(j, carry):
        cols = lanes(j, BLK)
        grad = gf[own, cols]
        for k in range(1, R):
            ga_send(j, k).wait_recv()
            grad = grad + gr[k - 1, :, cols].astype(F32)
        both = hf[own, lanes(j, PAIR)]
        gate, up = both[:, :BLK], both[:, BLK:]
        sig = jax.nn.sigmoid(gate)
        gg = (grad * up * sig * (1.0 + gate * (1.0 - sig))).astype(BF16)
        gu = (grad * gate * sig).astype(BF16)
        gc[own, lanes(j, PAIR)] = jnp.concatenate([gg, gu], axis=1)
        for k in range(1, R):
            gc_send(j, k).start()
        return carry

    lax.fori_loop(0, nj, swiglu_back, 0)
    for q in range(NCH):
        stage_c(0, q)

    def gc_wait(j, carry):
        for k in range(1, R):
            at = gc.at[peer_rows(k), lanes(j, PAIR)]
            remote(at, at, gc_ss.at[k - 1, j], gc_rs.at[k - 1, j], {"row": row_at(k)}).wait_recv()
        return carry

    lax.fori_loop(0, nj, gc_wait, 0)
    gc_copy = pltpu.make_async_copy(gc, gc_out, o_sem.at[5])
    gc_copy.start()
    for q in range(NCH):
        stage_a(1, q)
        if q > 0:
            stage_b(1, q - 1)
        if q > 1:
            stage_c(1, q - 2)
    stage_b(1, NCH - 1)
    stage_c(1, NCH - 2)
    for q in range(NCH):
        stage_d(0, q)
    stage_c(1, NCH - 1)
    for q in range(NCH):
        stage_d(1, q)

    for a in range(2):
        for k in range(1, C):
            gather(a, 0, k).wait_send()
        for slot in range(1, 4):
            for k in range(C):
                gather(a, slot, k).wait_send()
        for q in range(NCH):
            send1(a, q, 0).wait_send()
            send1(a, q, 1).wait_send()
            send2(a, q).wait_send()
            for k in range(1, C):
                send3(a, q, k).wait_send()

    def drain(j, carry):
        for k in range(1, R):
            h_send(j, k).wait_send()
            act_send(j, k).wait_send()
            ga_send(j, k).wait_send()
            gc_send(j, k).wait_send()
        return carry

    lax.fori_loop(0, nj, drain, 0)
    x_copy.wait()
    g_copy.wait()
    act_copy.wait()
    gc_copy.wait()


def weight_grads(x_ref, g_ref, act_ref, gc_ref, kcat, kd, dg_ref, du_ref, dd_ref):
    width = x_ref.shape[1]
    nj = act_ref.shape[1] // BLK
    for j in range(nj):
        cols = slice(j * PAIR, (j + 1) * PAIR)
        value = lax.dot_general(x_ref[...], gc_ref[:, cols], TN, preferred_element_type=F32)
        value = value.astype(BF16)
        out = slice(j * BLK, (j + 1) * BLK)
        for i in range(width // BLK):
            at = slice(i * BLK, (i + 1) * BLK)
            block = masked(value[at], kcat[0, i : i + 1, cols])
            dg_ref[at, out] = block[:, :BLK]
            du_ref[at, out] = block[:, BLK:]
        down = lax.dot_general(act_ref[:, out], g_ref[...], TN, preferred_element_type=F32)
        dd_ref[out, :] = masked(down.astype(BF16), kd[j : j + 1, :])


def local(R, C, tokens, gate_weight, up_weight, down_weight, gate_mask, up_mask, down_mask, grad_out):
    rows, dl = tokens.shape
    hid = gate_weight.shape[1]
    total = rows * C * 4
    nj, ni = hid // BLK, dl // BLK
    half = total // R
    kcat = jnp.stack([gate_mask, up_mask], axis=2).reshape(ni, 2 * nj)
    kcat = jnp.repeat(kcat.astype(F32), BLK, axis=1)
    kd = jnp.repeat(down_mask.astype(F32), BLK, axis=1)
    any_spec = pl.BlockSpec(memory_space=pl.ANY)
    vmem = pl.BlockSpec(memory_space=pltpu.VMEM)
    part = (rows * C, dl)
    dma = pltpu.SemaphoreType.DMA
    S = jax.ShapeDtypeStruct
    mixed, gtok, x_all, g_all, act, gc = pl.pallas_call(
        functools.partial(fused, R, C),
        out_shape=(
            S((rows, dl), BF16), S((rows, dl), BF16), S((total, dl), BF16), S((total, dl), BF16),
            S((total, hid), BF16), S((total, 2 * hid), BF16),
        ),
        in_specs=[any_spec] * 5 + [vmem] * 2,
        out_specs=(vmem, vmem, any_spec, any_spec, any_spec, any_spec),
        scratch_shapes=[
            pltpu.VMEM((total, dl), BF16),
            pltpu.VMEM((total, dl), BF16),
            pltpu.VMEM((dl, 2 * hid), BF16),
            pltpu.VMEM((hid, dl), BF16),
            pltpu.VMEM((total, hid), BF16),
            pltpu.VMEM((total, 2 * hid), BF16),
            pltpu.VMEM((total, 2 * hid), F32),
            pltpu.VMEM((total, 2 * hid), BF16),
            pltpu.VMEM((R - 1, half, 2 * hid), BF16),
            pltpu.VMEM((total, hid), F32),
            pltpu.VMEM((total, hid), BF16),
            pltpu.VMEM((R - 1, half, hid), BF16),
            pltpu.VMEM((2, 4) + part, BF16),
            pltpu.VMEM((2, 2) + part, BF16),
            pltpu.VMEM((2,) + part, BF16),
            pltpu.VMEM((2,) + part, BF16),
            pltpu.VMEM((2,) + part, BF16),
            pltpu.VMEM((2, C - 1, rows, dl), BF16),
            dma((2, 4, C)), dma((2, 4, C)), dma((3, nj)),
            dma((R - 1, nj)), dma((R - 1, nj)), dma((R - 1, nj)), dma((R - 1, nj)),
            dma((R - 1, nj)), dma((R - 1, nj)), dma((R - 1, nj)), dma((R - 1, nj)),
            dma((2, NCH, 2 + C)), dma((2, NCH, 2 + C)), dma((6,)),
        ],
        compiler_params=pltpu.CompilerParams(
            collective_id=0, has_side_effects=True, vmem_limit_bytes=60 * 2**20
        ),
        name="layer",
    )(tokens, grad_out, gate_weight, up_weight, down_weight, kcat, kd)

    width = 512
    whole = lambda i: (0, 0)
    dg, du, dd = pl.pallas_call(
        weight_grads,
        grid=(dl // width,),
        out_shape=(S((dl, hid), BF16), S((dl, hid), BF16), S((hid, dl), BF16)),
        in_specs=[
            pl.BlockSpec((total, width), lambda i: (0, i)),
            pl.BlockSpec((total, width), lambda i: (0, i)),
            pl.BlockSpec((total, hid), whole),
            pl.BlockSpec((total, 2 * hid), whole),
            pl.BlockSpec((1, width // BLK, 2 * hid), lambda i: (i, 0, 0)),
            pl.BlockSpec((nj, width), lambda i: (0, i)),
        ],
        out_specs=(
            pl.BlockSpec((width, hid), lambda i: (i, 0)),
            pl.BlockSpec((width, hid), lambda i: (i, 0)),
            pl.BlockSpec((hid, width), lambda i: (0, i)),
        ),
        compiler_params=pltpu.CompilerParams(vmem_limit_bytes=60 * 2**20),
        name="weight_grads",
    )(x_all, g_all, act, gc, kcat.reshape(dl // width, width // BLK, 2 * hid), kd)
    return (mixed, gtok, dg, du, dd)


def solution(mesh):
    return jax.shard_map(
        functools.partial(local, mesh.shape["row"], mesh.shape["col"]),
        mesh=mesh,
        in_specs=(
            P(("col", "depth"), "row"),
            P("row", ("col", "depth")),
            P("row", ("col", "depth")),
            P(("col", "depth"), "row"),
            P("row", ("col", "depth")),
            P("row", ("col", "depth")),
            P(("col", "depth"), "row"),
            P(("col", "depth"), "row"),
        ),
        out_specs=(
            P(("col", "depth"), "row"),
            P(("col", "depth"), "row"),
            P("row", ("col", "depth")),
            P("row", ("col", "depth")),
            P(("col", "depth"), "row"),
        ),
        check_vma=False,
    )
```

```python
import functools

import jax
import jax.numpy as jnp
from jax import lax
from jax.experimental import pallas as pl
from jax.experimental.pallas import tpu as pltpu
from jax.sharding import PartitionSpec as P

BLK = 128
PAIR = 2 * BLK
NCH = 4
F32 = jnp.float32
BF16 = jnp.bfloat16
MESH = pl.DeviceIdType.MESH
NT = (((1,), (1,)), ((), ()))
TN = (((0,), (0,)), ((), ()))


def masked(block, *keeps):
    rows, lanes = block.shape
    keep = [jnp.full((16, BLK), k, jnp.int32).astype(F32).astype(BF16) for k in keeps]
    keep = jnp.concatenate(keep, axis=1)
    return (block.reshape(rows // 16, 16, lanes) * keep[None]).reshape(rows, lanes)


def fused(
    R, C,
    x_hbm, g_hbm, wg_hbm, wu_hbm, wd_hbm, kg, ku, kd,
    mixed, gtok, x_out, g_out, act_out, gc_out,
    x_all, g_all, wcat, wd, act, gc, hf, hb, hr, gf, gb, gr, part, r1, s1, r2, zb, r3,
    a_ss, a_rs, w_sem, h_ss, h_rs, act_ss, act_rs, ga_ss, ga_rs, gc_ss, gc_rs, q_ss, q_rs, o_sem,
):
    r, c, d = lax.axis_index("row"), lax.axis_index("col"), lax.axis_index("depth")
    rows, dl = x_hbm.shape
    tokens = x_all.shape[0]
    nj = wd.shape[0] // BLK
    ni = dl // BLK
    half = tokens // R
    ch = dl // NCH
    d1 = d + 1 - 2 * lax.rem(d, 2)
    d2 = lax.rem(d + 2, 4)
    d3 = lax.rem(d1 + 2, 4)
    own = pl.ds(pl.multiple_of(r * half, half), half)

    def remote(src, dst, ss, rs, dev):
        return pltpu.make_async_remote_copy(
            src_ref=src, dst_ref=dst, send_sem=ss, recv_sem=rs, device_id=dev, device_id_type=MESH
        )

    def col_at(k):
        return lax.rem(c + k, C)

    def row_at(k):
        return lax.rem(r + k, R)

    barrier = pltpu.get_barrier_semaphore()
    peers = [{"col": col_at(k)} for k in range(1, C)]
    peers += [{"row": row_at(k)} for k in range(1, R)]
    peers += [{"depth": d1}, {"depth": d2}]
    for dev in peers:
        pl.semaphore_signal(barrier, inc=1, device_id=dev, device_id_type=MESH)
    pl.semaphore_wait(barrier, len(peers))

    srcs, alls = (x_hbm, g_hbm), (x_all, g_all)

    def blk(cc, dd):
        return pl.ds(pl.multiple_of((cc * 4 + dd) * rows, rows), rows)

    def hop(a, slot, k):
        if slot == 1:
            dev, at = {"depth": d2}, blk(col_at(C - k), d)
        elif slot == 2:
            dev, at = {"depth": d1}, blk(col_at(C - k), d)
        else:
            dev, at = {"depth": d1}, blk(col_at(C - k), d2)
        src = srcs[a] if k == 0 and slot < 3 else alls[a].at[at]
        return remote(src, alls[a].at[at], a_ss.at[a, slot, k], a_rs.at[a, slot, k], dev)

    def arrived(a, slot, k):
        dd = (d, d2, d1, d3, d2)[slot]
        at = blk(col_at(C - k), dd)
        remote(
            alls[a].at[at], alls[a].at[at], a_ss.at[a, slot, k], a_rs.at[a, slot, k], {"depth": d1}
        ).wait_recv()

    def chain(a, slot, way, k):
        index = k if way > 0 else C - k
        back = k - 1 if way > 0 else C - k + 1
        at = blk(col_at(C - back), d if slot == 0 else d2)
        src = srcs[a] if slot == 0 and k == 1 else alls[a].at[at]
        dev = {"col": col_at(1 if way > 0 else C - 1)}
        return remote(
            src, alls[a].at[at], a_ss.at[a, slot, index], a_rs.at[a, slot, index], dev
        )

    def chain_sends(way, k):
        if way > 0:
            return jnp.logical_and(c >= k - 1, c < C - 1)
        return jnp.logical_and(c + k - 1 <= C - 1, c > 0)

    def chain_start(a, slot, k, way):
        @pl.when(chain_sends(way, k))
        def _():
            chain(a, slot, way, k).start()

    def chain_step(a, slot, k, onward):
        for way in (1, -1):
            here = c >= k if way > 0 else c + k <= C - 1
            index = k if way > 0 else C - k

            @pl.when(here)
            def _():
                arrived(a, slot, index)
                if k < C - 1:
                    chain_start(a, slot, k + 1, way)
                for other in onward:
                    hop(a, other, index).start()

    def local_own(a):
        return pltpu.make_async_copy(srcs[a], alls[a].at[blk(c, d)], o_sem.at[a])

    def gather_last(a):
        local_own(a).wait()
        for k in range(C):
            arrived(a, 2, k)
        for k in range(C):
            arrived(a, 3, k)

    def lanes(j, width):
        return pl.ds(pl.multiple_of(j * width, width), width)

    def w_copies(j):
        left = pl.ds(pl.multiple_of(j * PAIR, BLK), BLK)
        right = pl.ds(pl.multiple_of(j * PAIR + BLK, BLK), BLK)
        return (
            pltpu.make_async_copy(wg_hbm.at[:, lanes(j, BLK)], wcat.at[:, left], w_sem.at[0, j]),
            pltpu.make_async_copy(wu_hbm.at[:, lanes(j, BLK)], wcat.at[:, right], w_sem.at[1, j]),
        )

    def d_copy(j):
        return pltpu.make_async_copy(
            wd_hbm.at[lanes(j, BLK), :], wd.at[lanes(j, BLK), :], w_sem.at[2, j]
        )

    for way in (1, -1):
        chain_start(0, 0, 1, way)
    hop(0, 1, 0).start()
    hop(1, 1, 0).start()
    hop(0, 2, 0).start()
    local_own(0).start()
    for j in range(nj):
        for copy in w_copies(j):
            copy.start()
    for j in range(nj):
        d_copy(j).start()

    def mask_cat(j, carry):
        for copy in w_copies(j):
            copy.wait()
        cols = lanes(j, PAIR)

        def one(i, inner):
            at = lanes(i, BLK)
            wcat[at, cols] = masked(wcat[at, cols], kg[j, i], ku[j, i])
            return inner

        return lax.fori_loop(0, ni, one, carry)

    def mask_down(j, carry):
        d_copy(j).wait()

        def one(i, inner):
            at = lanes(i, PAIR)
            wd[lanes(j, BLK), at] = masked(wd[lanes(j, BLK), at], kd[j, 2 * i], kd[j, 2 * i + 1])
            return inner

        return lax.fori_loop(0, ni // 2, one, carry)

    cuts = [nj * n // 3 for n in range(4)]
    chain_step(0, 0, 1, (1, 2))
    for way in (1, -1):
        chain_start(1, 0, 1, way)
    hop(1, 2, 0).start()
    local_own(1).start()
    arrived(1, 1, 0)
    for way in (1, -1):
        chain_start(1, 4, 1, way)
    hop(1, 3, 0).start()
    lax.fori_loop(cuts[0], cuts[1], mask_cat, 0)
    for k in range(2, C):
        chain_step(0, 0, k, (1, 2))
        chain_step(1, 0, k - 1, (2,))
        chain_step(1, 4, k - 1, (3,))
    lax.fori_loop(cuts[1], cuts[2], mask_cat, 0)
    for k in range(C):
        arrived(0, 1, k)
        hop(0, 3, k).start()
    lax.fori_loop(cuts[2], cuts[3], mask_cat, 0)
    gather_last(0)

    def h_send(j, k):
        at = pl.ds(pl.multiple_of(row_at(k) * half, half), half)
        return remote(
            hb.at[at, lanes(j, PAIR)], hr.at[k - 1, :, lanes(j, PAIR)],
            h_ss.at[k - 1, j], h_rs.at[k - 1, j], {"row": row_at(k)},
        )

    def hidden(j, carry):
        cols = lanes(j, PAIR)
        value = jnp.dot(x_all[...], wcat[:, cols], preferred_element_type=F32)
        hf[:, cols] = value
        hb[:, cols] = value.astype(BF16)
        for k in range(1, R):
            h_send(j, k).start()
        return carry

    lax.fori_loop(0, nj // 2, hidden, 0)
    chain_step(1, 0, C - 1, (2,))
    chain_step(1, 4, C - 1, (3,))
    lax.fori_loop(nj // 2, nj, hidden, 0)
    x_copy = pltpu.make_async_copy(x_all, x_out, o_sem.at[2])
    x_copy.start()
    lax.fori_loop(0, nj, mask_down, 0)

    def act_send(j, k):
        at = act.at[own, lanes(j, BLK)]
        return remote(at, at, act_ss.at[k - 1, j], act_rs.at[k - 1, j], {"row": row_at(k)})

    def activate(j, carry):
        cols = lanes(j, PAIR)
        total = hf[own, cols]
        for k in range(1, R):
            h_send(j, k).wait_recv()
            total = total + hr[k - 1, :, cols].astype(F32)
        hf[own, cols] = total
        gate, up = total[:, :BLK], total[:, BLK:]
        act[own, lanes(j, BLK)] = (gate * jax.nn.sigmoid(gate) * up).astype(BF16)
        for k in range(1, R):
            act_send(j, k).start()
        return carry

    lax.fori_loop(0, nj, activate, 0)
    gather_last(1)
    g_copy = pltpu.make_async_copy(g_all, g_out, o_sem.at[3])
    g_copy.start()

    def ga_send(j, k):
        at = pl.ds(pl.multiple_of(row_at(k) * half, half), half)
        return remote(
            gb.at[at, lanes(j, BLK)], gr.at[k - 1, :, lanes(j, BLK)],
            ga_ss.at[k - 1, j], ga_rs.at[k - 1, j], {"row": row_at(k)},
        )

    def back(j, carry):
        cols = lanes(j, BLK)
        value = lax.dot_general(g_all[...], wd[cols, :], NT, preferred_element_type=F32)
        gf[:, cols] = value
        gb[:, cols] = value.astype(BF16)
        for k in range(1, R):
            ga_send(j, k).start()
        return carry

    lax.fori_loop(0, nj, back, 0)

    def peer_rows(k):
        return pl.ds(pl.multiple_of(row_at(R - k) * half, half), half)

    def act_wait(j, carry):
        for k in range(1, R):
            at = act.at[peer_rows(k), lanes(j, BLK)]
            remote(at, at, act_ss.at[k - 1, j], act_rs.at[k - 1, j], {"row": row_at(k)}).wait_recv()
        return carry

    lax.fori_loop(0, nj, act_wait, 0)
    act_copy = pltpu.make_async_copy(act, act_out, o_sem.at[4])
    act_copy.start()

    outs = (mixed, gtok)

    def send1(a, q, h):
        cols = pl.ds(q * ch, ch)
        dst = (d1, d3)[h]
        return remote(
            part.at[a, dst, :, cols], r1.at[a, h, :, cols],
            q_ss.at[a, q, h], q_rs.at[a, q, h], {"depth": d1},
        )

    def send2(a, q):
        cols = pl.ds(q * ch, ch)
        return remote(
            s1.at[a, :, cols], r2.at[a, :, cols], q_ss.at[a, q, 2], q_rs.at[a, q, 2], {"depth": d2}
        )

    def send3(a, q, k):
        cols = pl.ds(q * ch, ch)
        at = pl.ds(pl.multiple_of(col_at(k) * rows, rows), rows)
        return remote(
            zb.at[a, at, cols], r3.at[a, k - 1, :, cols],
            q_ss.at[a, q, 2 + k], q_rs.at[a, q, 2 + k], {"col": col_at(k)},
        )

    def stage_a(a, q):
        def tile(n, carry):
            cols = pl.ds(pl.multiple_of(q * ch + n * PAIR, PAIR), PAIR)
            if a == 0:
                value = jnp.dot(act[...], wd[:, cols], preferred_element_type=F32)
            else:
                value = lax.dot_general(gc[...], wcat[cols, :], NT, preferred_element_type=F32)
            value = value.astype(BF16)
            for cc in range(C):
                for dd in range(4):
                    at = (cc * 4 + dd) * rows
                    part[a, dd, cc * rows : (cc + 1) * rows, cols] = value[at : at + rows]
            return carry

        lax.fori_loop(0, ch // PAIR, tile, 0)
        send1(a, q, 1).start()
        send1(a, q, 0).start()

    def stage_b(a, q):
        cols = pl.ds(q * ch, ch)
        send1(a, q, 1).wait_recv()
        s1[a, :, cols] = (part[a, d2, :, cols].astype(F32) + r1[a, 1, :, cols].astype(F32)).astype(BF16)
        send2(a, q).start()

    def stage_c(a, q):
        cols = pl.ds(q * ch, ch)
        send1(a, q, 0).wait_recv()
        send2(a, q).wait_recv()
        total = part[a, d, :, cols].astype(F32) + r1[a, 0, :, cols].astype(F32)
        zb[a, :, cols] = (total + r2[a, :, cols].astype(F32)).astype(BF16)
        for k in range(C - 1, 0, -1):
            send3(a, q, k).start()

    def stage_d(a, q):
        cols = pl.ds(q * ch, ch)
        at = pl.ds(pl.multiple_of(c * rows, rows), rows)
        total = zb[a, at, cols].astype(F32)
        for k in range(1, C):
            send3(a, q, k).wait_recv()
            total = total + r3[a, k - 1, :, cols].astype(F32)
        outs[a][:, cols] = total.astype(BF16)

    for q in range(NCH):
        stage_a(0, q)
        if q > 0:
            stage_b(0, q - 1)
    stage_b(0, NCH - 1)

    def gc_send(j, k):
        at = gc.at[own, lanes(j, PAIR)]
        return remote(at, at, gc_ss.at[k - 1, j], gc_rs.at[k - 1, j], {"row": row_at(k)})

    def swiglu_back(j, carry):
        cols = lanes(j, BLK)
        grad = gf[own, cols]
        for k in range(1, R):
            ga_send(j, k).wait_recv()
            grad = grad + gr[k - 1, :, cols].astype(F32)
        both = hf[own, lanes(j, PAIR)]
        gate, up = both[:, :BLK], both[:, BLK:]
        sig = jax.nn.sigmoid(gate)
        gg = (grad * up * sig * (1.0 + gate * (1.0 - sig))).astype(BF16)
        gu = (grad * gate * sig).astype(BF16)
        gc[own, lanes(j, PAIR)] = jnp.concatenate([gg, gu], axis=1)
        for k in range(1, R):
            gc_send(j, k).start()
        return carry

    lax.fori_loop(0, nj, swiglu_back, 0)
    for q in range(NCH):
        stage_c(0, q)

    def gc_wait(j, carry):
        for k in range(1, R):
            at = gc.at[peer_rows(k), lanes(j, PAIR)]
            remote(at, at, gc_ss.at[k - 1, j], gc_rs.at[k - 1, j], {"row": row_at(k)}).wait_recv()
        return carry

    lax.fori_loop(0, nj, gc_wait, 0)
    gc_copy = pltpu.make_async_copy(gc, gc_out, o_sem.at[5])
    gc_copy.start()
    for q in range(NCH):
        stage_a(1, q)
        if q > 0:
            stage_b(1, q - 1)
        if q > 1:
            stage_c(1, q - 2)
    stage_b(1, NCH - 1)
    stage_c(1, NCH - 2)
    for q in range(NCH):
        stage_d(0, q)
    stage_c(1, NCH - 1)
    for q in range(NCH):
        stage_d(1, q)

    for a in range(2):
        for slot in (0, 4) if a == 1 else (0,):
            for way in (1, -1):
                for k in range(1, C):

                    @pl.when(chain_sends(way, k))
                    def _():
                        chain(a, slot, way, k).wait_send()

        for k in range(C):
            if a == 0 or k == 0:
                hop(a, 1, k).wait_send()
            hop(a, 2, k).wait_send()
            hop(a, 3, k).wait_send()
        for q in range(NCH):
            send1(a, q, 0).wait_send()
            send1(a, q, 1).wait_send()
            send2(a, q).wait_send()
            for k in range(1, C):
                send3(a, q, k).wait_send()

    def drain(j, carry):
        for k in range(1, R):
            h_send(j, k).wait_send()
            act_send(j, k).wait_send()
            ga_send(j, k).wait_send()
            gc_send(j, k).wait_send()
        return carry

    lax.fori_loop(0, nj, drain, 0)
    x_copy.wait()
    g_copy.wait()
    act_copy.wait()
    gc_copy.wait()


def weight_grads(
    x_ref, g_ref, act_ref, gc_ref, kg, ku, kd, mixed_in, gtok_in, dg_ref, du_ref, dd_ref, mixed, gtok
):
    width = x_ref.shape[1]
    first = pl.program_id(0) * (width // BLK)
    nj = act_ref.shape[1] // BLK
    mixed[...] = mixed_in[...]
    gtok[...] = gtok_in[...]
    for j in range(nj):
        cols = slice(j * PAIR, (j + 1) * PAIR)
        value = lax.dot_general(x_ref[...], gc_ref[:, cols], TN, preferred_element_type=F32)
        value = value.astype(BF16)
        out = slice(j * BLK, (j + 1) * BLK)
        down = lax.dot_general(act_ref[:, out], g_ref[...], TN, preferred_element_type=F32)
        down = down.astype(BF16)
        for i in range(width // BLK):
            at = slice(i * BLK, (i + 1) * BLK)
            block = masked(value[at], kg[j, first + i], ku[j, first + i])
            dg_ref[at, out] = block[:, :BLK]
            du_ref[at, out] = block[:, BLK:]
            dd_ref[out, at] = masked(down[:, at], kd[j, first + i])


def local(R, C, tokens, gate_weight, up_weight, down_weight, gate_mask, up_mask, down_mask, grad_out):
    rows, dl = tokens.shape
    hid = gate_weight.shape[1]
    total = rows * C * 4
    nj = hid // BLK
    half = total // R
    masks = (gate_mask.T, up_mask.T, down_mask)
    smem = pl.BlockSpec(memory_space=pltpu.SMEM)
    any_spec = pl.BlockSpec(memory_space=pl.ANY)
    vmem = pl.BlockSpec(memory_space=pltpu.VMEM)
    part = (rows * C, dl)
    dma = pltpu.SemaphoreType.DMA
    S = jax.ShapeDtypeStruct
    mixed, gtok, x_all, g_all, act, gc = pl.pallas_call(
        functools.partial(fused, R, C),
        out_shape=(
            S((rows, dl), BF16), S((rows, dl), BF16), S((total, dl), BF16), S((total, dl), BF16),
            S((total, hid), BF16), S((total, 2 * hid), BF16),
        ),
        in_specs=[any_spec] * 5 + [smem] * 3,
        out_specs=(vmem, vmem, any_spec, any_spec, any_spec, any_spec),
        scratch_shapes=[
            pltpu.VMEM((total, dl), BF16),
            pltpu.VMEM((total, dl), BF16),
            pltpu.VMEM((dl, 2 * hid), BF16),
            pltpu.VMEM((hid, dl), BF16),
            pltpu.VMEM((total, hid), BF16),
            pltpu.VMEM((total, 2 * hid), BF16),
            pltpu.VMEM((total, 2 * hid), F32),
            pltpu.VMEM((total, 2 * hid), BF16),
            pltpu.VMEM((R - 1, half, 2 * hid), BF16),
            pltpu.VMEM((total, hid), F32),
            pltpu.VMEM((total, hid), BF16),
            pltpu.VMEM((R - 1, half, hid), BF16),
            pltpu.VMEM((2, 4) + part, BF16),
            pltpu.VMEM((2, 2) + part, BF16),
            pltpu.VMEM((2,) + part, BF16),
            pltpu.VMEM((2,) + part, BF16),
            pltpu.VMEM((2,) + part, BF16),
            pltpu.VMEM((2, C - 1, rows, dl), BF16),
            dma((2, 5, C)), dma((2, 5, C)), dma((3, nj)),
            dma((R - 1, nj)), dma((R - 1, nj)), dma((R - 1, nj)), dma((R - 1, nj)),
            dma((R - 1, nj)), dma((R - 1, nj)), dma((R - 1, nj)), dma((R - 1, nj)),
            dma((2, NCH, 2 + C)), dma((2, NCH, 2 + C)), dma((6,)),
        ],
        compiler_params=pltpu.CompilerParams(
            collective_id=0, has_side_effects=True, vmem_limit_bytes=60 * 2**20
        ),
        name="layer",
    )(tokens, grad_out, gate_weight, up_weight, down_weight, *masks)

    width = 512
    whole = lambda i: (0, 0)
    dg, du, dd, mixed, gtok = pl.pallas_call(
        weight_grads,
        grid=(dl // width,),
        out_shape=(
            S((dl, hid), BF16), S((dl, hid), BF16), S((hid, dl), BF16),
            S((rows, dl), BF16), S((rows, dl), BF16),
        ),
        in_specs=[
            pl.BlockSpec((total, width), lambda i: (0, i)),
            pl.BlockSpec((total, width), lambda i: (0, i)),
            pl.BlockSpec((total, hid), whole),
            pl.BlockSpec((total, 2 * hid), whole),
            smem,
            smem,
            smem,
            pl.BlockSpec((rows, width), lambda i: (0, i)),
            pl.BlockSpec((rows, width), lambda i: (0, i)),
        ],
        out_specs=(
            pl.BlockSpec((width, hid), lambda i: (i, 0)),
            pl.BlockSpec((width, hid), lambda i: (i, 0)),
            pl.BlockSpec((hid, width), lambda i: (0, i)),
            pl.BlockSpec((rows, width), lambda i: (0, i)),
            pl.BlockSpec((rows, width), lambda i: (0, i)),
        ),
        compiler_params=pltpu.CompilerParams(vmem_limit_bytes=60 * 2**20),
        name="weight_grads",
    )(x_all, g_all, act, gc, *masks, mixed, gtok)
    return (mixed, gtok, dg, du, dd)


def solution(mesh):
    return jax.shard_map(
        functools.partial(local, mesh.shape["row"], mesh.shape["col"]),
        mesh=mesh,
        in_specs=(
            P(("col", "depth"), "row"),
            P("row", ("col", "depth")),
            P("row", ("col", "depth")),
            P(("col", "depth"), "row"),
            P("row", ("col", "depth")),
            P("row", ("col", "depth")),
            P(("col", "depth"), "row"),
            P(("col", "depth"), "row"),
        ),
        out_specs=(
            P(("col", "depth"), "row"),
            P(("col", "depth"), "row"),
            P("row", ("col", "depth")),
            P("row", ("col", "depth")),
            P(("col", "depth"), "row"),
        ),
        check_vma=False,
    )
```

```python
import functools

import jax
import jax.numpy as jnp
from jax import lax
from jax.experimental import pallas as pl
from jax.experimental.pallas import tpu as pltpu
from jax.sharding import PartitionSpec as P

BLK = 128
PAIR = 2 * BLK
NCH = 4
F32 = jnp.float32
BF16 = jnp.bfloat16
MESH = pl.DeviceIdType.MESH
NT = (((1,), (1,)), ((), ()))
TN = (((0,), (0,)), ((), ()))


def masked(block, *keeps):
    rows, lanes = block.shape
    keep = [jnp.full((16, BLK), k, jnp.int32).astype(F32).astype(BF16) for k in keeps]
    keep = jnp.concatenate(keep, axis=1)
    return (block.reshape(rows // 16, 16, lanes) * keep[None]).reshape(rows, lanes)


def fused(
    R, C,
    x_hbm, g_hbm, wg_hbm, wu_hbm, wd_hbm, kg, ku, kd,
    mixed, gtok, x_out, g_out, act_out, gc_out,
    x_all, g_all, wcat, wd, act, gc, hf, hb, hr, gf, gb, gr, part, r1, s1, r2, zb, r3,
    a_ss, a_rs, w_sem, h_ss, h_rs, act_ss, act_rs, ga_ss, ga_rs, gc_ss, gc_rs, q_ss, q_rs, o_sem,
):
    r, c, d = lax.axis_index("row"), lax.axis_index("col"), lax.axis_index("depth")
    rows, dl = x_hbm.shape
    tokens = x_all.shape[0]
    nj = wd.shape[0] // BLK
    ni = dl // BLK
    half = tokens // R
    ch = dl // NCH
    d1 = d + 1 - 2 * lax.rem(d, 2)
    d2 = lax.rem(d + 2, 4)
    d3 = lax.rem(d1 + 2, 4)
    own = pl.ds(pl.multiple_of(r * half, half), half)

    def remote(src, dst, ss, rs, dev):
        return pltpu.make_async_remote_copy(
            src_ref=src, dst_ref=dst, send_sem=ss, recv_sem=rs, device_id=dev, device_id_type=MESH
        )

    def col_at(k):
        return lax.rem(c + k, C)

    def row_at(k):
        return lax.rem(r + k, R)

    barrier = pltpu.get_barrier_semaphore()
    peers = [{"col": col_at(k)} for k in range(1, C)]
    peers += [{"row": row_at(k)} for k in range(1, R)]
    peers += [{"depth": d1}, {"depth": d2}]
    for dev in peers:
        pl.semaphore_signal(barrier, inc=1, device_id=dev, device_id_type=MESH)
    pl.semaphore_wait(barrier, len(peers))

    srcs, alls = (x_hbm, g_hbm), (x_all, g_all)

    def blk(cc, dd):
        return pl.ds(pl.multiple_of((cc * 4 + dd) * rows, rows), rows)

    def hop(a, slot, k):
        if slot == 1:
            dev, at = {"depth": d2}, blk(col_at(C - k), d)
        elif slot == 2:
            dev, at = {"depth": d1}, blk(col_at(C - k), d)
        else:
            dev, at = {"depth": d1}, blk(col_at(C - k), d2)
        src = srcs[a] if k == 0 and slot < 3 else alls[a].at[at]
        return remote(src, alls[a].at[at], a_ss.at[a, slot, k], a_rs.at[a, slot, k], dev)

    def arrived(a, slot, k):
        dd = (d, d2, d1, d3, d2)[slot]
        at = blk(col_at(C - k), dd)
        remote(
            alls[a].at[at], alls[a].at[at], a_ss.at[a, slot, k], a_rs.at[a, slot, k], {"depth": d1}
        ).wait_recv()

    def chain(a, slot, way, k):
        index = k if way > 0 else C - k
        back = k - 1 if way > 0 else C - k + 1
        at = blk(col_at(C - back), d if slot == 0 else d2)
        src = srcs[a] if slot == 0 and k == 1 else alls[a].at[at]
        dev = {"col": col_at(1 if way > 0 else C - 1)}
        return remote(
            src, alls[a].at[at], a_ss.at[a, slot, index], a_rs.at[a, slot, index], dev
        )

    def chain_sends(way, k):
        if way > 0:
            return jnp.logical_and(c >= k - 1, c < C - 1)
        return jnp.logical_and(c + k - 1 <= C - 1, c > 0)

    def chain_start(a, slot, k, way):
        @pl.when(chain_sends(way, k))
        def _():
            chain(a, slot, way, k).start()

    def chain_step(a, slot, k, onward):
        for way in (1, -1):
            here = c >= k if way > 0 else c + k <= C - 1
            index = k if way > 0 else C - k

            @pl.when(here)
            def _():
                arrived(a, slot, index)
                if k < C - 1:
                    chain_start(a, slot, k + 1, way)
                for other in onward:
                    hop(a, other, index).start()

    def local_own(a):
        return pltpu.make_async_copy(srcs[a], alls[a].at[blk(c, d)], o_sem.at[a])

    def gather_last(a):
        local_own(a).wait()
        for k in range(C):
            arrived(a, 2, k)
        for k in range(C):
            arrived(a, 3, k)

    def lanes(j, width):
        return pl.ds(pl.multiple_of(j * width, width), width)

    def w_copies(j):
        left = pl.ds(pl.multiple_of(j * PAIR, BLK), BLK)
        right = pl.ds(pl.multiple_of(j * PAIR + BLK, BLK), BLK)
        return (
            pltpu.make_async_copy(wg_hbm.at[:, lanes(j, BLK)], wcat.at[:, left], w_sem.at[0, j]),
            pltpu.make_async_copy(wu_hbm.at[:, lanes(j, BLK)], wcat.at[:, right], w_sem.at[1, j]),
        )

    def d_copy(j):
        return pltpu.make_async_copy(
            wd_hbm.at[lanes(j, BLK), :], wd.at[lanes(j, BLK), :], w_sem.at[2, j]
        )

    for way in (1, -1):
        chain_start(0, 0, 1, way)
    hop(0, 1, 0).start()
    hop(1, 1, 0).start()
    hop(0, 2, 0).start()
    local_own(0).start()
    for j in range(nj):
        for copy in w_copies(j):
            copy.start()
    for j in range(nj):
        d_copy(j).start()

    def mask_cat(j, carry):
        for copy in w_copies(j):
            copy.wait()
        cols = lanes(j, PAIR)

        def one(i, inner):
            at = lanes(i, BLK)
            wcat[at, cols] = masked(wcat[at, cols], kg[j, i], ku[j, i])
            return inner

        return lax.fori_loop(0, ni, one, carry)

    def mask_down(j, carry):
        d_copy(j).wait()

        def one(i, inner):
            at = lanes(i, PAIR)
            wd[lanes(j, BLK), at] = masked(wd[lanes(j, BLK), at], kd[j, 2 * i], kd[j, 2 * i + 1])
            return inner

        return lax.fori_loop(0, ni // 2, one, carry)

    cuts = [nj * n // 3 for n in range(4)]
    chain_step(0, 0, 1, (1, 2))
    for way in (1, -1):
        chain_start(1, 0, 1, way)
    hop(1, 2, 0).start()
    local_own(1).start()
    arrived(1, 1, 0)
    for way in (1, -1):
        chain_start(1, 4, 1, way)
    hop(1, 3, 0).start()
    lax.fori_loop(cuts[0], cuts[1], mask_cat, 0)
    for k in range(2, C):
        chain_step(0, 0, k, (1, 2))
        chain_step(1, 0, k - 1, (2,))
        chain_step(1, 4, k - 1, (3,))
    lax.fori_loop(cuts[1], cuts[2], mask_cat, 0)
    for k in range(C):
        arrived(0, 1, k)
        hop(0, 3, k).start()
    lax.fori_loop(cuts[2], cuts[3], mask_cat, 0)
    lax.fori_loop(0, nj, mask_down, 0)
    gather_last(0)

    def h_send(j, k):
        at = pl.ds(pl.multiple_of(row_at(k) * half, half), half)
        return remote(
            hb.at[at, lanes(j, PAIR)], hr.at[k - 1, :, lanes(j, PAIR)],
            h_ss.at[k - 1, j], h_rs.at[k - 1, j], {"row": row_at(k)},
        )

    def hidden(j, carry):
        cols = lanes(j, PAIR)
        value = jnp.dot(x_all[...], wcat[:, cols], preferred_element_type=F32)
        hf[:, cols] = value
        hb[:, cols] = value.astype(BF16)
        for k in range(1, R):
            h_send(j, k).start()
        return carry

    lax.fori_loop(0, nj // 2, hidden, 0)
    chain_step(1, 0, C - 1, (2,))
    chain_step(1, 4, C - 1, (3,))
    lax.fori_loop(nj // 2, nj, hidden, 0)
    x_copy = pltpu.make_async_copy(x_all, x_out, o_sem.at[2])
    x_copy.start()

    def act_send(j, k):
        at = act.at[own, lanes(j, BLK)]
        return remote(at, at, act_ss.at[k - 1, j], act_rs.at[k - 1, j], {"row": row_at(k)})

    def activate(j, carry):
        cols = lanes(j, PAIR)
        total = hf[own, cols]
        for k in range(1, R):
            h_send(j, k).wait_recv()
            total = total + hr[k - 1, :, cols].astype(F32)
        hf[own, cols] = total
        gate, up = total[:, :BLK], total[:, BLK:]
        act[own, lanes(j, BLK)] = (gate * jax.nn.sigmoid(gate) * up).astype(BF16)
        for k in range(1, R):
            act_send(j, k).start()
        return carry

    gather_last(1)
    g_copy = pltpu.make_async_copy(g_all, g_out, o_sem.at[3])
    g_copy.start()

    def ga_send(j, k):
        at = pl.ds(pl.multiple_of(row_at(k) * half, half), half)
        return remote(
            gb.at[at, lanes(j, BLK)], gr.at[k - 1, :, lanes(j, BLK)],
            ga_ss.at[k - 1, j], ga_rs.at[k - 1, j], {"row": row_at(k)},
        )

    def back(j, carry):
        cols = lanes(j, BLK)
        value = lax.dot_general(g_all[...], wd[cols, :], NT, preferred_element_type=F32)
        gf[:, cols] = value
        gb[:, cols] = value.astype(BF16)
        for k in range(1, R):
            ga_send(j, k).start()
        return carry

    lax.fori_loop(0, nj, back, 0)
    lax.fori_loop(0, nj, activate, 0)

    def peer_rows(k):
        return pl.ds(pl.multiple_of(row_at(R - k) * half, half), half)

    def act_wait(j, carry):
        for k in range(1, R):
            at = act.at[peer_rows(k), lanes(j, BLK)]
            remote(at, at, act_ss.at[k - 1, j], act_rs.at[k - 1, j], {"row": row_at(k)}).wait_recv()
        return carry

    def gc_send(j, k):
        at = gc.at[own, lanes(j, PAIR)]
        return remote(at, at, gc_ss.at[k - 1, j], gc_rs.at[k - 1, j], {"row": row_at(k)})

    def swiglu_back(j, carry):
        cols = lanes(j, BLK)
        grad = gf[own, cols]
        for k in range(1, R):
            ga_send(j, k).wait_recv()
            grad = grad + gr[k - 1, :, cols].astype(F32)
        both = hf[own, lanes(j, PAIR)]
        gate, up = both[:, :BLK], both[:, BLK:]
        sig = jax.nn.sigmoid(gate)
        gg = (grad * up * sig * (1.0 + gate * (1.0 - sig))).astype(BF16)
        gu = (grad * gate * sig).astype(BF16)
        gc[own, lanes(j, PAIR)] = jnp.concatenate([gg, gu], axis=1)
        for k in range(1, R):
            gc_send(j, k).start()
        return carry

    lax.fori_loop(0, nj, swiglu_back, 0)
    lax.fori_loop(0, nj, act_wait, 0)
    act_copy = pltpu.make_async_copy(act, act_out, o_sem.at[4])
    act_copy.start()

    outs = (mixed, gtok)

    def send1(a, q, h):
        cols = pl.ds(q * ch, ch)
        dst = (d1, d3)[h]
        return remote(
            part.at[a, dst, :, cols], r1.at[a, h, :, cols],
            q_ss.at[a, q, h], q_rs.at[a, q, h], {"depth": d1},
        )

    def send2(a, q):
        cols = pl.ds(q * ch, ch)
        return remote(
            s1.at[a, :, cols], r2.at[a, :, cols], q_ss.at[a, q, 2], q_rs.at[a, q, 2], {"depth": d2}
        )

    def send3(a, q, k):
        cols = pl.ds(q * ch, ch)
        at = pl.ds(pl.multiple_of(col_at(k) * rows, rows), rows)
        return remote(
            zb.at[a, at, cols], r3.at[a, k - 1, :, cols],
            q_ss.at[a, q, 2 + k], q_rs.at[a, q, 2 + k], {"col": col_at(k)},
        )

    def stage_a(a, q):
        def tile(n, carry):
            cols = pl.ds(pl.multiple_of(q * ch + n * PAIR, PAIR), PAIR)
            if a == 0:
                value = jnp.dot(act[...], wd[:, cols], preferred_element_type=F32)
            else:
                value = lax.dot_general(gc[...], wcat[cols, :], NT, preferred_element_type=F32)
            value = value.astype(BF16)
            for cc in range(C):
                for dd in range(4):
                    at = (cc * 4 + dd) * rows
                    part[a, dd, cc * rows : (cc + 1) * rows, cols] = value[at : at + rows]
            return carry

        lax.fori_loop(0, ch // PAIR, tile, 0)
        send1(a, q, 1).start()
        send1(a, q, 0).start()

    def stage_b(a, q):
        cols = pl.ds(q * ch, ch)
        send1(a, q, 1).wait_recv()
        s1[a, :, cols] = (part[a, d2, :, cols].astype(F32) + r1[a, 1, :, cols].astype(F32)).astype(BF16)
        send2(a, q).start()

    def stage_c(a, q):
        cols = pl.ds(q * ch, ch)
        send1(a, q, 0).wait_recv()
        send2(a, q).wait_recv()
        total = part[a, d, :, cols].astype(F32) + r1[a, 0, :, cols].astype(F32)
        zb[a, :, cols] = (total + r2[a, :, cols].astype(F32)).astype(BF16)
        for k in range(C - 1, 0, -1):
            send3(a, q, k).start()

    def stage_d(a, q):
        cols = pl.ds(q * ch, ch)
        at = pl.ds(pl.multiple_of(c * rows, rows), rows)
        total = zb[a, at, cols].astype(F32)
        for k in range(1, C):
            send3(a, q, k).wait_recv()
            total = total + r3[a, k - 1, :, cols].astype(F32)
        outs[a][:, cols] = total.astype(BF16)

    for q in range(NCH):
        stage_a(0, q)
        if q > 0:
            stage_b(0, q - 1)
    stage_b(0, NCH - 1)

    for q in range(NCH):
        stage_c(0, q)

    def gc_wait(j, carry):
        for k in range(1, R):
            at = gc.at[peer_rows(k), lanes(j, PAIR)]
            remote(at, at, gc_ss.at[k - 1, j], gc_rs.at[k - 1, j], {"row": row_at(k)}).wait_recv()
        return carry

    lax.fori_loop(0, nj, gc_wait, 0)
    gc_copy = pltpu.make_async_copy(gc, gc_out, o_sem.at[5])
    gc_copy.start()
    for q in range(NCH):
        stage_a(1, q)
        if q > 0:
            stage_b(1, q - 1)
        if q > 1:
            stage_c(1, q - 2)
    stage_b(1, NCH - 1)
    stage_c(1, NCH - 2)
    for q in range(NCH):
        stage_d(0, q)
    stage_c(1, NCH - 1)
    for q in range(NCH):
        stage_d(1, q)

    for a in range(2):
        for slot in (0, 4) if a == 1 else (0,):
            for way in (1, -1):
                for k in range(1, C):

                    @pl.when(chain_sends(way, k))
                    def _():
                        chain(a, slot, way, k).wait_send()

        for k in range(C):
            if a == 0 or k == 0:
                hop(a, 1, k).wait_send()
            hop(a, 2, k).wait_send()
            hop(a, 3, k).wait_send()
        for q in range(NCH):
            send1(a, q, 0).wait_send()
            send1(a, q, 1).wait_send()
            send2(a, q).wait_send()
            for k in range(1, C):
                send3(a, q, k).wait_send()

    def drain(j, carry):
        for k in range(1, R):
            h_send(j, k).wait_send()
            act_send(j, k).wait_send()
            ga_send(j, k).wait_send()
            gc_send(j, k).wait_send()
        return carry

    lax.fori_loop(0, nj, drain, 0)
    x_copy.wait()
    g_copy.wait()
    act_copy.wait()
    gc_copy.wait()


def weight_grads(
    x_ref, g_ref, act_ref, gc_ref, kg, ku, kd, mixed_in, gtok_in, dg_ref, du_ref, dd_ref, mixed, gtok
):
    width = x_ref.shape[1]
    first = pl.program_id(0) * (width // BLK)
    nj = act_ref.shape[1] // BLK
    mixed[...] = mixed_in[...]
    gtok[...] = gtok_in[...]
    for j in range(nj):
        cols = slice(j * PAIR, (j + 1) * PAIR)
        value = lax.dot_general(x_ref[...], gc_ref[:, cols], TN, preferred_element_type=F32)
        value = value.astype(BF16)
        out = slice(j * BLK, (j + 1) * BLK)
        down = lax.dot_general(act_ref[:, out], g_ref[...], TN, preferred_element_type=F32)
        down = down.astype(BF16)
        for i in range(width // BLK):
            at = slice(i * BLK, (i + 1) * BLK)
            block = masked(value[at], kg[j, first + i], ku[j, first + i])
            dg_ref[at, out] = block[:, :BLK]
            du_ref[at, out] = block[:, BLK:]
            dd_ref[out, at] = masked(down[:, at], kd[j, first + i])


def local(R, C, tokens, gate_weight, up_weight, down_weight, gate_mask, up_mask, down_mask, grad_out):
    rows, dl = tokens.shape
    hid = gate_weight.shape[1]
    total = rows * C * 4
    nj = hid // BLK
    half = total // R
    masks = (gate_mask.T, up_mask.T, down_mask)
    smem = pl.BlockSpec(memory_space=pltpu.SMEM)
    any_spec = pl.BlockSpec(memory_space=pl.ANY)
    vmem = pl.BlockSpec(memory_space=pltpu.VMEM)
    part = (rows * C, dl)
    dma = pltpu.SemaphoreType.DMA
    S = jax.ShapeDtypeStruct
    mixed, gtok, x_all, g_all, act, gc = pl.pallas_call(
        functools.partial(fused, R, C),
        out_shape=(
            S((rows, dl), BF16), S((rows, dl), BF16), S((total, dl), BF16), S((total, dl), BF16),
            S((total, hid), BF16), S((total, 2 * hid), BF16),
        ),
        in_specs=[any_spec] * 5 + [smem] * 3,
        out_specs=(vmem, vmem, any_spec, any_spec, any_spec, any_spec),
        scratch_shapes=[
            pltpu.VMEM((total, dl), BF16),
            pltpu.VMEM((total, dl), BF16),
            pltpu.VMEM((dl, 2 * hid), BF16),
            pltpu.VMEM((hid, dl), BF16),
            pltpu.VMEM((total, hid), BF16),
            pltpu.VMEM((total, 2 * hid), BF16),
            pltpu.VMEM((total, 2 * hid), F32),
            pltpu.VMEM((total, 2 * hid), BF16),
            pltpu.VMEM((R - 1, half, 2 * hid), BF16),
            pltpu.VMEM((total, hid), F32),
            pltpu.VMEM((total, hid), BF16),
            pltpu.VMEM((R - 1, half, hid), BF16),
            pltpu.VMEM((2, 4) + part, BF16),
            pltpu.VMEM((2, 2) + part, BF16),
            pltpu.VMEM((2,) + part, BF16),
            pltpu.VMEM((2,) + part, BF16),
            pltpu.VMEM((2,) + part, BF16),
            pltpu.VMEM((2, C - 1, rows, dl), BF16),
            dma((2, 5, C)), dma((2, 5, C)), dma((3, nj)),
            dma((R - 1, nj)), dma((R - 1, nj)), dma((R - 1, nj)), dma((R - 1, nj)),
            dma((R - 1, nj)), dma((R - 1, nj)), dma((R - 1, nj)), dma((R - 1, nj)),
            dma((2, NCH, 2 + C)), dma((2, NCH, 2 + C)), dma((6,)),
        ],
        compiler_params=pltpu.CompilerParams(
            collective_id=0, has_side_effects=True, vmem_limit_bytes=60 * 2**20
        ),
        name="layer",
    )(tokens, grad_out, gate_weight, up_weight, down_weight, *masks)

    width = 512
    whole = lambda i: (0, 0)
    dg, du, dd, mixed, gtok = pl.pallas_call(
        weight_grads,
        grid=(dl // width,),
        out_shape=(
            S((dl, hid), BF16), S((dl, hid), BF16), S((hid, dl), BF16),
            S((rows, dl), BF16), S((rows, dl), BF16),
        ),
        in_specs=[
            pl.BlockSpec((total, width), lambda i: (0, i)),
            pl.BlockSpec((total, width), lambda i: (0, i)),
            pl.BlockSpec((total, hid), whole),
            pl.BlockSpec((total, 2 * hid), whole),
            smem,
            smem,
            smem,
            pl.BlockSpec((rows, width), lambda i: (0, i)),
            pl.BlockSpec((rows, width), lambda i: (0, i)),
        ],
        out_specs=(
            pl.BlockSpec((width, hid), lambda i: (i, 0)),
            pl.BlockSpec((width, hid), lambda i: (i, 0)),
            pl.BlockSpec((hid, width), lambda i: (0, i)),
            pl.BlockSpec((rows, width), lambda i: (0, i)),
            pl.BlockSpec((rows, width), lambda i: (0, i)),
        ),
        compiler_params=pltpu.CompilerParams(vmem_limit_bytes=60 * 2**20),
        name="weight_grads",
    )(x_all, g_all, act, gc, *masks, mixed, gtok)
    return (mixed, gtok, dg, du, dd)


def solution(mesh):
    return jax.shard_map(
        functools.partial(local, mesh.shape["row"], mesh.shape["col"]),
        mesh=mesh,
        in_specs=(
            P(("col", "depth"), "row"),
            P("row", ("col", "depth")),
            P("row", ("col", "depth")),
            P(("col", "depth"), "row"),
            P("row", ("col", "depth")),
            P("row", ("col", "depth")),
            P(("col", "depth"), "row"),
            P(("col", "depth"), "row"),
        ),
        out_specs=(
            P(("col", "depth"), "row"),
            P(("col", "depth"), "row"),
            P("row", ("col", "depth")),
            P("row", ("col", "depth")),
            P(("col", "depth"), "row"),
        ),
        check_vma=False,
    )
```
